512 devices in a mesh: row: 16 (over y_lo, x, core), col: 32 (over z, y_hi).
Axes of the slice: x: 4, y: 4 (y_hi: 2, y_lo: 2; y = y_hi * 2 + y_lo), z: 16, core: 2. Of those that a mesh axis runs over, the one named last changes fastest.
Arguments:
- fitted_ac: bfloat16 [1600, 16, 4096], P('row', None, 'col'), may hold values from -6 to 6
- fitted_bd: bfloat16 [1600, 8, 4096], P('row', None, 'col'), may hold values from -0.1875 to 0.1875
- amplitudes: bfloat16 [4, 16, 8], P(None, 'row'), may hold values from -0.5 to 0.5
Outputs:
- ladder: float32 [4, 1600, 1600], P(None, 'row', 'col')
The draws below stay inside these ranges and needn't reach their ends.
All inputs are finite; a program needn't handle non-finite values.
Results may differ from the reference program's by a relative error of at most 0.0029.
Values may be sent and summed in bfloat16 or wider, within the bound.
No kernel may reach another device: no remote copies, remote signals or barrier semaphores. Data moves between devices by JAX's collectives and lax.ppermute only.
A program may use at most 128 MiB of HBM per device.

```python
import jax
import jax.numpy as jnp
from jax import lax

V = 1600
NQ = 4096
P_SIZE = 4
CW = 16
DW = 8
N_ROW = 16


def spiked(values, stream_key, source, target, blocks, factor):
    owner, partner = [(jnp.arange(values.shape[axis_at]) // (values.shape[axis_at] // blocks)).reshape([-1 if axis == axis_at else 1 for axis in range(values.ndim)]) for axis_at in (source, target)]
    chosen = jax.random.permutation(stream_key, blocks)[partner]
    strong = (owner == chosen) | (owner == (partner + blocks // 2) % blocks)
    return jnp.where(strong, factor * values, values)


def level_of(stream_key, dims, split, low, high):
    def one(dim, parts):
        heights = jax.random.uniform(jax.random.fold_in(jax.random.fold_in(stream_key, 6), dim), (parts,), jnp.float32, low / len(split), high / len(split))
        return jnp.repeat(jnp.exp(heights), dims[dim] // parts).reshape((-1,) + (1,) * (len(dims) - dim - 1))

    factor_of = one(*split[0])
    for cut in split[1:]:
        factor_of = factor_of * one(*cut)
    return factor_of


def scatter_about(key, extent, width, limit, cuts=(), held_as=jnp.bfloat16):
    result = jax.random.normal(key, extent, jnp.float32) * width
    if len(cuts) > 0:
        result = level_of(key, extent, cuts, -0.22, 0.18) * result
    return jnp.clip(result, min=-limit, max=limit).astype(held_as)


def bell_draw_with(own_key, dims, spread, most, shards, heavy, held_as=jnp.bfloat16):
    drawn = spread * jax.random.normal(own_key, dims, jnp.float32)
    if shards:
        drawn = drawn * level_of(own_key, dims, shards, -0.22, 0.18)
    return jnp.clip(spiked(drawn, jax.random.fold_in(own_key, 3), *heavy), -most, most).astype(held_as)


def setup_inputs(seed: int = 0) -> dict:
    streams_of = jax.random.split(jax.random.key(seed), 4)
    return {
        "fitted_ac": scatter_about(streams_of[0], (V, CW, NQ), 1.0, 6.0, ((0, 16), (2, 32))),
        "fitted_bd": bell_draw_with(streams_of[1], (V, DW, NQ), NQ ** -0.5, 0.1875, ((0, 16), (2, 32)), (2, 0, 32, 2.75)),
        "amplitudes": scatter_about(streams_of[2], (P_SIZE, CW, DW), (CW * DW) ** -0.5, 0.5, ((1, 16),)),
    }


def reference(fitted_ac, fitted_bd, amplitudes):
    left_full = fitted_ac.astype(jnp.float32)
    amp_full = amplitudes.astype(jnp.float32)
    blocks = fitted_bd.reshape(N_ROW, V // N_ROW, DW, NQ)

    def one_block(block):
        half = jnp.einsum("bdq,pcd->bpcq", block.astype(jnp.float32), amp_full).astype(jnp.bfloat16)
        half = lax.optimization_barrier(half)
        return jnp.einsum("acq,bpcq->pab", left_full, half.astype(jnp.float32))

    pieces = lax.map(one_block, blocks)
    return jnp.transpose(pieces, (1, 2, 0, 3)).reshape(P_SIZE, V, V)
```

```python
import jax
import jax.numpy as jnp
from jax import lax
from jax.experimental import pallas as pl
from jax.experimental.pallas import tpu as pltpu
from jax.sharding import Mesh, PartitionSpec as P

ROW = ("yl", "xh", "xl", "core")
COL = ("zq", "zl", "yh")
NT = (((1,), (1,)), ((), ()))
MIB = 1024 * 1024

NA, NB, C, D, NP, Q = 100, 100, 16, 8, 4, 128
ROWS = NA * NP
PAD = 112
PIECE = 160
CHUNKS = (0, 16, 32, 48, 64, 80, 84)


def x_kernel(w_ref, ac_ref, x_ref):
    for a0 in CHUNKS:
        y = jnp.dot(
            w_ref[...], ac_ref[0, a0 * C:(a0 + 16) * C, :], preferred_element_type=jnp.float32
        )
        high = y.astype(jnp.bfloat16)
        low = (y - high.astype(jnp.float32)).astype(jnp.bfloat16)
        for d in range(D):
            rows = slice(a0 * NP, (a0 + 16) * NP)
            x_ref[0, 0, rows, d * Q:(d + 1) * Q] = high[64 * d:64 * (d + 1)]
            x_ref[0, 1, rows, d * Q:(d + 1) * Q] = low[64 * d:64 * (d + 1)]


def make_x(w, ac):
    return pl.pallas_call(
        x_kernel,
        grid=(4,),
        in_specs=[
            pl.BlockSpec((512, 256), lambda k: (0, 0)),
            pl.BlockSpec((1, NA * C, Q), lambda k: (k, 0, 0)),
        ],
        out_specs=pl.BlockSpec((1, 2, ROWS, D * Q), lambda k: (k, 0, 0, 0)),
        out_shape=jax.ShapeDtypeStruct((4, 2, ROWS, D * Q), jnp.bfloat16),
        compiler_params=pltpu.CompilerParams(vmem_limit_bytes=32 * MIB),
        cost_estimate=pl.CostEstimate(flops=2 * 28 * 512 * 256 * 128, bytes_accessed=9 * MIB, transcendentals=0),
        name="make_x",
    )(w, ac)


def product(bd_ref, x_ref):
    left = bd_ref[...].reshape(4 * PAD, 512)
    return lax.dot_general(left, x_ref[0, 0], NT, preferred_element_type=jnp.float32) + lax.dot_general(
        left, x_ref[0, 1], NT, preferred_element_type=jnp.float32
    )


def first_kernel(core_ref, bd_ref, x_ref, acc_ref):
    value = product(bd_ref, x_ref)
    k = pl.program_id(0)

    @pl.when(k == 0)
    def _():
        acc_ref[...] = value

    @pl.when(k > 0)
    def _():
        acc_ref[...] += value


def second_kernel(core_ref, bd_ref, x_ref, before_ref, out_ref, acc_ref, piece_ref):
    value = product(bd_ref, x_ref)
    k = pl.program_id(0)

    @pl.when(k == 0)
    def _():
        acc_ref[...] = before_ref[...] + value

    @pl.when(k > 0)
    def _():
        acc_ref[...] += value

    @pl.when(k == 3)
    def _():
        for t in range(4):
            for yh in range(2):
                at = t * PAD + 50 * yh
                for j in range(3):
                    piece_ref[50 * j:50 * j + 50, :] = acc_ref[at:at + 50, 128 * j:128 * (j + 1)]
                rest = [acc_ref[at + 10 * g:at + 10 * g + 10, 384:400] for g in range(5)]
                piece_ref[150:160, :] = jnp.concatenate(rest + [jnp.zeros((10, 48), jnp.float32)], axis=1)
                out_ref[2 * t + yh] = piece_ref[...].astype(jnp.bfloat16)


def multiply(core, bd, x, before=None):
    bd_spec = pl.BlockSpec((4, None, PAD, 512), lambda k, core_ref: (0, k // 2, 0, k % 2))
    x_spec = pl.BlockSpec((1, 2, ROWS, 512), lambda k, core_ref: (2 * (k // 2) + core_ref[0], 0, 0, k % 2))
    acc_spec = pl.BlockSpec((4 * PAD, ROWS), lambda k, core_ref: (0, 0))
    acc_shape = jax.ShapeDtypeStruct((4 * PAD, ROWS), jnp.float32)
    cost = pl.CostEstimate(flops=2 * 2 * 400 * 400 * 2048, bytes_accessed=6 * MIB, transcendentals=0)
    params = pltpu.CompilerParams(vmem_limit_bytes=32 * MIB)
    if before is None:
        return pl.pallas_call(
            first_kernel,
            grid_spec=pltpu.PrefetchScalarGridSpec(
                num_scalar_prefetch=1, grid=(4,), in_specs=[bd_spec, x_spec], out_specs=acc_spec
            ),
            out_shape=acc_shape,
            compiler_params=params,
            cost_estimate=cost,
            name="first_half",
        )(core, bd, x)
    return pl.pallas_call(
        second_kernel,
        grid_spec=pltpu.PrefetchScalarGridSpec(
            num_scalar_prefetch=1,
            grid=(4,),
            in_specs=[bd_spec, x_spec, acc_spec],
            out_specs=pl.BlockSpec((8, PIECE, 128), lambda k, core_ref: (0, 0, 0)),
            scratch_shapes=[pltpu.VMEM((4 * PAD, ROWS), jnp.float32), pltpu.VMEM((PIECE, 128), jnp.float32)],
        ),
        out_shape=jax.ShapeDtypeStruct((8, PIECE, 128), jnp.bfloat16),
        compiler_params=params,
        cost_estimate=cost,
        name="second_half",
    )(core, bd, x, before)


def last_kernel(parts_ref, out_ref, sum_ref, turned_ref):
    sum_ref[...] = jnp.sum(parts_ref[...].astype(jnp.float32), axis=0)
    for j in range(3):
        turned_ref[128 * j:128 * (j + 1), :] = sum_ref[50 * j:50 * j + 50, :].T
    rest = sum_ref[150:160, :].T
    for g in range(5):
        turned_ref[384:400, 10 * g:10 * g + 10] = rest[16 * g:16 * (g + 1), :]
    for p in range(NP):
        out_ref[p] = turned_ref[pl.ds(p, NA, stride=NP), :]


def finish(parts):
    return pl.pallas_call(
        last_kernel,
        in_specs=[pl.BlockSpec(memory_space=pltpu.VMEM)],
        out_specs=pl.BlockSpec(memory_space=pltpu.VMEM),
        out_shape=jax.ShapeDtypeStruct((NP, NA, 50), jnp.float32),
        scratch_shapes=[pltpu.VMEM((PIECE, 128), jnp.float32), pltpu.VMEM((ROWS, 50), jnp.float32)],
        name="finish",
    )(parts)


def on_device(fitted_ac, fitted_bd, amplitudes):
    core = lax.axis_index("core").astype(jnp.int32)
    turn = [(4 * u + v, 4 * v + u) for u in range(4) for v in range(4)]
    mine = lax.ppermute(fitted_bd.reshape(NB, D * Q), ("xl", "core", "zl"), turn)
    ac_all = lax.all_to_all(
        jnp.broadcast_to(fitted_ac[None], (4,) + fitted_ac.shape), "zl", 0, 0, tiled=True
    ).reshape(4, NA * C, Q)
    bd_own = lax.all_to_all(
        jnp.broadcast_to(mine[None], (8,) + mine.shape), ("yl", "xh", "xl"), 0, 0, tiled=True
    )
    amp = lax.all_gather(amplitudes, ROW, axis=1, tiled=True)
    w = (
        jnp.transpose(amp, (2, 0, 1))[:, None, :, None, :] * jnp.eye(16, dtype=amp.dtype)[None, :, None, :, None]
    ).reshape(512, 256)
    x = make_x(w, ac_all)
    bd_other = lax.ppermute(bd_own, "core", [(0, 1), (1, 0)])
    acc = multiply(core[None], bd_own.reshape(4, 2, NB, D * Q), x)
    pieces = multiply((1 - core)[None], bd_other.reshape(4, 2, NB, D * Q), x, acc)
    return finish(lax.all_to_all(pieces, ("zq", "yh"), 0, 0, tiled=True))


def solution(mesh):
    fine = Mesh(mesh.devices.reshape(2, 2, 2, 2, 4, 4, 2), ROW + COL)
    return jax.shard_map(
        on_device,
        mesh=fine,
        in_specs=(P(ROW, None, COL), P(ROW, None, COL), P(None, ROW, None)),
        out_specs=P(None, ROW, COL),
        check_vma=False,
    )
```

```python
import jax
import jax.numpy as jnp
from jax import lax
from jax.experimental import pallas as pl
from jax.experimental.pallas import tpu as pltpu
from jax.sharding import Mesh, PartitionSpec as P

ROW = ("yl", "x", "core")
COL = ("zh", "zp", "yh")
NT = (((1,), (1,)), ((), ()))
MIB = 1024 * 1024

NA, NB, C, D, NP, Q = 100, 100, 16, 8, 4, 128
ROWS = NA * NP
HALF = 50
UNIT = 56
PAD = 64
PIECE = 160


def spread(amp, wide):
    tall, across = D * NP * wide, wide * C
    row = lax.broadcasted_iota(jnp.int32, (tall, D * NP), 0)
    col = lax.broadcasted_iota(jnp.int32, (tall, D * NP), 1)
    pick_row = jnp.where(row // wide == col, 1.0, 0.0).astype(jnp.bfloat16)
    row = lax.broadcasted_iota(jnp.int32, (C, across), 0)
    col = lax.broadcasted_iota(jnp.int32, (C, across), 1)
    pick_col = jnp.where(col % C == row, 1.0, 0.0).astype(jnp.bfloat16)
    wider = jnp.dot(pick_row, amp.T, preferred_element_type=jnp.float32).astype(jnp.bfloat16)
    full = jnp.dot(wider, pick_col, preferred_element_type=jnp.float32)
    row = lax.broadcasted_iota(jnp.int32, (tall, across), 0)
    col = lax.broadcasted_iota(jnp.int32, (tall, across), 1)
    return jnp.where(row % wide == col // C, full, 0.0).astype(jnp.bfloat16)


def product_kernel(m_ref, amp_ref, ac00_ref, ac01_ref, ac10_ref, ac11_ref, bd_ref, out_ref, ac_ref, x_ref, left_ref, acc_ref):
    for m, pair in enumerate(((ac00_ref, ac10_ref), (ac01_ref, ac11_ref))):

        @pl.when(m_ref[0] == m)
        def _():
            for dy in range(2):
                ac_ref[:, dy * Q:(dy + 1) * Q] = pair[dy][...]

    for dy in range(2):
        for t in range(8):
            left_ref[t, 0:UNIT, dy * D * Q:(dy + 1) * D * Q] = bd_ref[t, dy]
    w16, w4 = spread(amp_ref[...], 16), spread(amp_ref[...], 4)
    for k in range(7):
        w, n = (w16, 16) if k < 6 else (w4, 4)
        y = jnp.dot(w, ac_ref[k * 256:k * 256 + n * C, :], preferred_element_type=jnp.float32)
        high = y.astype(jnp.bfloat16)
        low = (y - high.astype(jnp.float32)).astype(jnp.bfloat16)
        tall = NP * n
        for dy in range(2):
            for d in range(D):
                rows, columns = slice(64 * k, 64 * k + tall), slice((dy * D + d) * Q, (dy * D + d + 1) * Q)
                here = slice(tall * d, tall * (d + 1)), slice(Q * dy, Q * (dy + 1))
                x_ref[0, rows, columns] = high[here]
                x_ref[1, rows, columns] = low[here]
    left = left_ref[...].reshape(8 * PAD, 2 * D * Q)
    acc_ref[...] = lax.dot_general(left, x_ref[0], NT, preferred_element_type=jnp.float32) + lax.dot_general(
        left, x_ref[1], NT, preferred_element_type=jnp.float32
    )
    for t in range(8):
        at = t * PAD
        for j in range(3):
            out_ref[t, 50 * j:50 * j + 50, :] = acc_ref[at:at + 50, 128 * j:128 * (j + 1)]
        rest = [acc_ref[at + 10 * g:at + 10 * g + 10, 384:400] for g in range(5)]
        out_ref[t, 150:160, :] = jnp.concatenate(rest + [jnp.zeros((10, 48), jnp.float32)], axis=1)


def multiply(m, amp, blocks, bd):
    return pl.pallas_call(
        product_kernel,
        in_specs=[pl.BlockSpec(memory_space=pltpu.SMEM)] + [pl.BlockSpec(memory_space=pltpu.VMEM)] * 6,
        out_specs=pl.BlockSpec(memory_space=pltpu.VMEM),
        scratch_shapes=[
            pltpu.VMEM((NA * C, 2 * Q), jnp.bfloat16),
            pltpu.VMEM((2, ROWS, 2 * D * Q), jnp.bfloat16),
            pltpu.VMEM((8, PAD, 2 * D * Q), jnp.bfloat16),
            pltpu.VMEM((8 * PAD, ROWS), jnp.float32),
        ],
        out_shape=jax.ShapeDtypeStruct((8, PIECE, 128), jnp.float32),
        compiler_params=pltpu.CompilerParams(vmem_limit_bytes=32 * MIB),
        cost_estimate=pl.CostEstimate(flops=2 * 2 * 400 * 400 * 2048, bytes_accessed=6 * MIB, transcendentals=0),
        name="multiply",
    )(m, amp, *blocks, bd)


def last_kernel(parts_ref, out_ref, sum_ref):
    sum_ref[...] = jnp.sum(parts_ref[...].astype(jnp.float32), axis=0)
    rest = jnp.concatenate([sum_ref[150:160, 16 * g:16 * (g + 1)] for g in range(5)], axis=0)
    for p in range(NP):
        pieces = [sum_ref[50 * (k // 2):50 * (k // 2) + 50, 64 * (k % 2) + 16 * p:64 * (k % 2) + 16 * p + 16] for k in range(6)]
        out_ref[:, p, :] = jnp.concatenate(pieces + [rest[:, 4 * p:4 * p + 4]], axis=1)


def finish(parts):
    return pl.pallas_call(
        last_kernel,
        in_specs=[pl.BlockSpec(memory_space=pltpu.VMEM)],
        out_specs=pl.BlockSpec(memory_space=pltpu.VMEM),
        out_shape=jax.ShapeDtypeStruct((50, NP, NA), jnp.float32),
        scratch_shapes=[pltpu.VMEM((PIECE, 128), jnp.float32)],
        name="finish",
    )(parts)


def on_device(fitted_ac, fitted_bd, amplitudes):
    core, zp, yh = (lax.axis_index(name) for name in ("core", "zp", "yh"))
    group = ("core", "zp", "yh")

    def sent(array, place):
        ways = []
        for e in range(2):
            for z in range(2):
                for y in range(2):
                    to = place(e, z, y)
                    ways.append((4 * e + 2 * z + y, 4 * to[0] + 2 * to[1] + to[2]))
        return lax.ppermute(array, group, ways)

    ac = fitted_ac.reshape(NA * C, Q)
    across = sent(ac, lambda e, z, y: (e, z, y ^ 1))
    blocks = [sent(array, lambda e, z, y: (z, e ^ m, y)) for array in (ac, across) for m in range(2)]

    halves = fitted_bd.reshape(2, HALF, D * Q)
    units = []
    for dy in range(2):
        half = lax.dynamic_index_in_dim(halves, yh ^ dy, 0, keepdims=False)
        half = jnp.pad(half, ((0, UNIT - HALF), (0, 0)))
        units.append(sent(half, lambda e, z, y: (z, e, y ^ dy)))
    flat = jnp.transpose(amplitudes, (1, 2, 0)).reshape(D * NP)
    peer = lax.ppermute(flat, "core", [(0, 1), (1, 0)])
    two = jnp.where(core == 0, jnp.concatenate([flat, peer]), jnp.concatenate([peer, flat]))
    both = jnp.stack(units) + jnp.pad(two[None, None], ((0, 1), (HALF, UNIT - HALF - 1), (0, D * Q - 2 * D * NP)))
    bd = lax.all_to_all(jnp.broadcast_to(both[None], (8,) + both.shape), ("yl", "x"), 0, 0, tiled=True)
    amp = bd[:, 0, HALF, :2 * D * NP].reshape(C, D * NP)

    m = (zp ^ core).astype(jnp.int32)[None]
    for_other = multiply(m ^ 1, amp, blocks, bd)
    for_self = multiply(m, amp, blocks, bd)
    pieces = (for_self + lax.ppermute(for_other, "core", [(0, 1), (1, 0)])).astype(jnp.bfloat16)
    summed = finish(lax.all_to_all(pieces, "zh", 0, 0, tiled=True))
    return jnp.transpose(summed, (1, 2, 0))


def solution(mesh):
    fine = Mesh(mesh.devices.reshape(2, 4, 2, 8, 2, 2), ROW + COL)
    return jax.shard_map(
        on_device,
        mesh=fine,
        in_specs=(P(ROW, None, COL), P(ROW, None, COL), P(None, ROW, None)),
        out_specs=P(None, ROW, COL),
        check_vma=False,
    )
```

```python
import jax
import jax.numpy as jnp
from jax import lax
from jax.experimental import pallas as pl
from jax.experimental.pallas import tpu as pltpu
from jax.sharding import Mesh, PartitionSpec as P

ROW = ("yl", "x", "core")
COL = ("zh", "zp", "yh")
NT = (((1,), (1,)), ((), ()))
MIB = 1024 * 1024

NA, NB, C, D, NP, Q = 100, 100, 16, 8, 4, 128
ROWS = NA * NP
HALF = 50
UNIT = 104
WIDE = 128
PIECE = 160


def spread(amp, wide):
    tall, across = D * NP * wide, wide * C
    row = lax.broadcasted_iota(jnp.int32, (tall, D * NP), 0)
    col = lax.broadcasted_iota(jnp.int32, (tall, D * NP), 1)
    pick_row = jnp.where(row // wide == col, 1.0, 0.0).astype(jnp.bfloat16)
    row = lax.broadcasted_iota(jnp.int32, (C, across), 0)
    col = lax.broadcasted_iota(jnp.int32, (C, across), 1)
    pick_col = jnp.where(col % C == row, 1.0, 0.0).astype(jnp.bfloat16)
    wider = jnp.dot(pick_row, amp.T, preferred_element_type=jnp.float32).astype(jnp.bfloat16)
    full = jnp.dot(wider, pick_col, preferred_element_type=jnp.float32)
    row = lax.broadcasted_iota(jnp.int32, (tall, across), 0)
    col = lax.broadcasted_iota(jnp.int32, (tall, across), 1)
    return jnp.where(row % wide == col // C, full, 0.0).astype(jnp.bfloat16)


def unit_kernel(one_ref, two_ref, amp_ref, later_ref, out_ref, unit_ref, sem_ref):
    unit_ref[0:HALF, :] = one_ref[...]
    unit_ref[HALF:2 * HALF, :] = two_ref[...]
    unit_ref[2 * HALF:, :] = jnp.zeros((UNIT - 2 * HALF, D * Q), jnp.bfloat16)
    unit_ref[2 * HALF:2 * HALF + 1, 0:2 * D * NP] = amp_ref[...]
    copies = [pltpu.make_async_copy(unit_ref, out_ref.at[t], sem_ref.at[t]) for t in range(8)]
    for copy in copies:
        copy.start()
    for copy in copies:
        copy.wait()


def make_unit(one, two, amp, later):
    inside, outside = pl.BlockSpec(memory_space=pltpu.VMEM), pl.BlockSpec(memory_space=pl.ANY)
    return pl.pallas_call(
        unit_kernel,
        in_specs=[inside, inside, inside, outside],
        out_specs=outside,
        out_shape=jax.ShapeDtypeStruct((8, UNIT, D * Q), jnp.bfloat16),
        scratch_shapes=[pltpu.VMEM((UNIT, D * Q), jnp.bfloat16), pltpu.SemaphoreType.DMA((8,))],
        name="make_unit",
    )(one, two, amp, later)


def product_kernel(m_ref, amp_ref, ac00_ref, ac01_ref, ac10_ref, ac11_ref, bd_ref, out_ref, ac_ref, x_ref, left_ref, acc_ref):
    for m, pair in enumerate(((ac00_ref, ac10_ref), (ac01_ref, ac11_ref))):

        @pl.when(m_ref[0] == m)
        def _():
            for dy in range(2):
                ac_ref[:, dy * Q:(dy + 1) * Q] = pair[dy][...]

    for dy in range(2):
        for t in range(8):
            left_ref[HALF * t:HALF * (t + 1), dy * D * Q:(dy + 1) * D * Q] = bd_ref[t, HALF * dy:HALF * (dy + 1), :]
    w16, w4 = spread(amp_ref[...], 16), spread(amp_ref[...], 4)
    for k in range(7):
        w, n = (w16, 16) if k < 6 else (w4, 4)
        y = jnp.dot(w, ac_ref[k * 256:k * 256 + n * C, :], preferred_element_type=jnp.float32)
        high = y.astype(jnp.bfloat16)
        low = (y - high.astype(jnp.float32)).astype(jnp.bfloat16)
        for dy in range(2):
            for d in range(D):
                for p in range(NP):
                    rows, columns = slice(WIDE * p + 16 * k, WIDE * p + 16 * k + n), slice((dy * D + d) * Q, (dy * D + d + 1) * Q)
                    here = slice(n * (d * NP + p), n * (d * NP + p + 1)), slice(Q * dy, Q * (dy + 1))
                    x_ref[0, rows, columns] = high[here]
                    x_ref[1, rows, columns] = low[here]
    acc_ref[...] = lax.dot_general(left_ref[...], x_ref[0], NT, preferred_element_type=jnp.float32) + lax.dot_general(
        left_ref[...], x_ref[1], NT, preferred_element_type=jnp.float32
    )
    for t in range(8):
        at = slice(HALF * t, HALF * (t + 1))
        last = acc_ref[at, 3 * WIDE:3 * WIDE + NA]
        for j in range(3):
            out_ref[t, 50 * j:50 * j + 50, :] = jnp.concatenate(
                [acc_ref[at, WIDE * j:WIDE * j + NA], last[:, 28 * j:28 * j + 28]], axis=1
            )
        rest = [last[10 * g:10 * g + 10, 84:100] for g in range(5)]
        out_ref[t, 150:160, :] = jnp.concatenate(rest + [jnp.zeros((10, 48), jnp.float32)], axis=1)


def multiply(m, amp, blocks, bd):
    return pl.pallas_call(
        product_kernel,
        in_specs=[pl.BlockSpec(memory_space=pltpu.SMEM)] + [pl.BlockSpec(memory_space=pltpu.VMEM)] * 6,
        out_specs=pl.BlockSpec(memory_space=pltpu.VMEM),
        scratch_shapes=[
            pltpu.VMEM((NA * C, 2 * Q), jnp.bfloat16),
            pltpu.VMEM((2, NP * WIDE, 2 * D * Q), jnp.bfloat16),
            pltpu.VMEM((8 * HALF, 2 * D * Q), jnp.bfloat16),
            pltpu.VMEM((8 * HALF, NP * WIDE), jnp.float32),
        ],
        out_shape=jax.ShapeDtypeStruct((8, PIECE, 128), jnp.float32),
        compiler_params=pltpu.CompilerParams(vmem_limit_bytes=32 * MIB),
        cost_estimate=pl.CostEstimate(flops=2 * 2 * 400 * 400 * 2048, bytes_accessed=6 * MIB, transcendentals=0),
        name="multiply",
    )(m, amp, *blocks, bd)


def last_kernel(parts_ref, out_ref, sum_ref):
    sum_ref[...] = jnp.sum(parts_ref[...].astype(jnp.float32), axis=0)
    for j in range(3):
        out_ref[:, j, :] = sum_ref[50 * j:50 * j + 50, 0:NA]
    rest = jnp.concatenate([sum_ref[150:160, 16 * g:16 * (g + 1)] for g in range(5)], axis=0)
    out_ref[:, 3, :] = jnp.concatenate([sum_ref[50 * j:50 * j + 50, NA:] for j in range(3)] + [rest], axis=1)


def finish(parts):
    return pl.pallas_call(
        last_kernel,
        in_specs=[pl.BlockSpec(memory_space=pltpu.VMEM)],
        out_specs=pl.BlockSpec(memory_space=pltpu.VMEM),
        out_shape=jax.ShapeDtypeStruct((50, NP, NA), jnp.float32),
        scratch_shapes=[pltpu.VMEM((PIECE, 128), jnp.float32)],
        name="finish",
    )(parts)


def on_device(fitted_ac, fitted_bd, amplitudes):
    core, zp, yh = (lax.axis_index(name) for name in ("core", "zp", "yh"))
    group = ("core", "zp", "yh")

    def sent(array, place):
        ways = []
        for e in range(2):
            for z in range(2):
                for y in range(2):
                    to = place(e, z, y)
                    ways.append((4 * e + 2 * z + y, 4 * to[0] + 2 * to[1] + to[2]))
        return lax.ppermute(array, group, ways)

    ac = fitted_ac.reshape(NA * C, Q)
    across = sent(ac, lambda e, z, y: (e, z, y ^ 1))
    blocks = [sent(array, lambda e, z, y: (z, e ^ m, y)) for array in (ac, across) for m in range(2)]

    halves = fitted_bd.reshape(2, HALF, D * Q)
    units = []
    for dy in range(2):
        half = lax.dynamic_index_in_dim(halves, yh ^ dy, 0, keepdims=False)
        units.append(sent(half, lambda e, z, y: (z, e, y ^ dy)))
    flat = jnp.transpose(amplitudes, (1, 2, 0)).reshape(1, D * NP)
    peer = lax.ppermute(flat, "core", [(0, 1), (1, 0)])
    two = jnp.where(core == 0, jnp.concatenate([flat, peer], axis=1), jnp.concatenate([peer, flat], axis=1))
    bd = lax.all_to_all(make_unit(*units, two, across), ("yl", "x"), 0, 0, tiled=True)
    amp = bd[:, 2 * HALF, :2 * D * NP].reshape(C, D * NP)

    m = (zp ^ core).astype(jnp.int32)[None]
    for_other = multiply(m ^ 1, amp, blocks, bd)
    for_self = multiply(m, amp, blocks, bd)
    pieces = (for_self + lax.ppermute(for_other, "core", [(0, 1), (1, 0)])).astype(jnp.bfloat16)
    summed = finish(lax.all_to_all(pieces, "zh", 0, 0, tiled=True))
    return jnp.transpose(summed, (1, 2, 0))


def solution(mesh):
    fine = Mesh(mesh.devices.reshape(2, 4, 2, 8, 2, 2), ROW + COL)
    return jax.shard_map(
        on_device,
        mesh=fine,
        in_specs=(P(ROW, None, COL), P(ROW, None, COL), P(None, ROW, None)),
        out_specs=P(None, ROW, COL),
        check_vma=False,
    )
```

```python
import jax
import jax.numpy as jnp
from jax import lax
from jax.experimental import pallas as pl
from jax.experimental.pallas import tpu as pltpu
from jax.sharding import Mesh, PartitionSpec as P

ROW = ("yl", "xh", "xl", "core")
COL = ("zq", "zl", "yh")
DELTA = ((2, 1), (0, 3))
HALF_OF = (1, 0, 0, 1)
NT = (((1,), (1,)), ((), ()))
MIB = 1024 * 1024

NA, NB, C, D, NP, Q = 100, 100, 16, 8, 4, 128
ROWS = NA * NP
HALF = 50
UNIT = 104
WIDE = 128
PIECE = 160


def spread(amp, wide):
    tall, across = D * NP * wide, wide * C
    row = lax.broadcasted_iota(jnp.int32, (tall, D * NP), 0)
    col = lax.broadcasted_iota(jnp.int32, (tall, D * NP), 1)
    pick_row = jnp.where(row // wide == col, 1.0, 0.0).astype(jnp.bfloat16)
    row = lax.broadcasted_iota(jnp.int32, (C, across), 0)
    col = lax.broadcasted_iota(jnp.int32, (C, across), 1)
    pick_col = jnp.where(col % C == row, 1.0, 0.0).astype(jnp.bfloat16)
    wider = jnp.dot(pick_row, amp.T, preferred_element_type=jnp.float32).astype(jnp.bfloat16)
    full = jnp.dot(wider, pick_col, preferred_element_type=jnp.float32)
    row = lax.broadcasted_iota(jnp.int32, (tall, across), 0)
    col = lax.broadcasted_iota(jnp.int32, (tall, across), 1)
    return jnp.where(row % wide == col // C, full, 0.0).astype(jnp.bfloat16)


def in_a_row(amp):
    row = lax.broadcasted_iota(jnp.int32, (D, D * NP), 0)
    col = lax.broadcasted_iota(jnp.int32, (D, D * NP), 1)
    pick = jnp.where(col // NP == row, 1.0, 0.0).astype(jnp.bfloat16)
    wide = jnp.dot(amp, pick, preferred_element_type=jnp.float32)
    row = lax.broadcasted_iota(jnp.int32, (NP, D * NP), 0)
    col = lax.broadcasted_iota(jnp.int32, (NP, D * NP), 1)
    return jnp.sum(jnp.where(col % NP == row, wide, 0.0), axis=0, keepdims=True)


def unit_kernel(core_ref, bd_ref, amp_ref, peer_ref, out_ref, wide_ref, unit_ref, sem_ref):
    wide_ref[...] = bd_ref[...].astype(jnp.float32).reshape(NB * D, Q)
    for d in range(D):
        unit_ref[0:NB, d * Q:(d + 1) * Q] = wide_ref[pl.ds(d, NB, stride=D), :].astype(jnp.bfloat16)
    unit_ref[NB:, :] = jnp.zeros((UNIT - NB, D * Q), jnp.bfloat16)
    own, peer = in_a_row(amp_ref[...]), in_a_row(peer_ref[...])
    first = core_ref[0] == 0
    both = jnp.concatenate([jnp.where(first, own, peer), jnp.where(first, peer, own)], axis=1)
    unit_ref[NB:NB + 1, 0:2 * D * NP] = both.astype(jnp.bfloat16)
    copies = [pltpu.make_async_copy(unit_ref, out_ref.at[t], sem_ref.at[t]) for t in range(8)]
    for copy in copies:
        copy.start()
    for copy in copies:
        copy.wait()


def make_unit(core, bd, amp, peer):
    inside, outside = pl.BlockSpec(memory_space=pltpu.VMEM), pl.BlockSpec(memory_space=pl.ANY)
    return pl.pallas_call(
        unit_kernel,
        in_specs=[pl.BlockSpec(memory_space=pltpu.SMEM), inside, inside, inside],
        out_specs=outside,
        out_shape=jax.ShapeDtypeStruct((8, UNIT, D * Q), jnp.bfloat16),
        scratch_shapes=[
            pltpu.VMEM((NB * D, Q), jnp.float32),
            pltpu.VMEM((UNIT, D * Q), jnp.bfloat16),
            pltpu.SemaphoreType.DMA((8,)),
        ],
        compiler_params=pltpu.CompilerParams(vmem_limit_bytes=16 * MIB),
        name="make_unit",
    )(core, bd, amp, peer)


def product_kernel(m_ref, amp_ref, ac00_ref, ac01_ref, ac10_ref, ac11_ref, bd_ref, out_ref, ac_ref, x_ref, left_ref, acc_ref):
    for m, pair in enumerate(((ac00_ref, ac10_ref), (ac01_ref, ac11_ref))):

        @pl.when(m_ref[0] == m)
        def _():
            for h in range(2):
                ac_ref[:, h * Q:(h + 1) * Q] = pair[h][...]

    for h in range(2):
        for t in range(4):
            left_ref[NB * t:NB * (t + 1), h * D * Q:(h + 1) * D * Q] = bd_ref[2 * t + h, 0:NB, :]
    w16, w4 = spread(amp_ref[...], 16), spread(amp_ref[...], 4)
    for k in range(7):
        w, n = (w16, 16) if k < 6 else (w4, 4)
        y = jnp.dot(w, ac_ref[k * 256:k * 256 + n * C, :], preferred_element_type=jnp.float32)
        high = y.astype(jnp.bfloat16)
        low = (y - high.astype(jnp.float32)).astype(jnp.bfloat16)
        for h in range(2):
            for d in range(D):
                for p in range(NP):
                    rows, columns = slice(WIDE * p + 16 * k, WIDE * p + 16 * k + n), slice((h * D + d) * Q, (h * D + d + 1) * Q)
                    here = slice(n * (d * NP + p), n * (d * NP + p + 1)), slice(Q * h, Q * (h + 1))
                    x_ref[0, rows, columns] = high[here]
                    x_ref[1, rows, columns] = low[here]
    acc_ref[...] = lax.dot_general(left_ref[...], x_ref[0], NT, preferred_element_type=jnp.float32) + lax.dot_general(
        left_ref[...], x_ref[1], NT, preferred_element_type=jnp.float32
    )
    for t in range(8):
        at = slice(HALF * t, HALF * (t + 1))
        last = acc_ref[at, 3 * WIDE:3 * WIDE + NA]
        for j in range(3):
            out_ref[t, 50 * j:50 * j + 50, :] = jnp.concatenate(
                [acc_ref[at, WIDE * j:WIDE * j + NA], last[:, 28 * j:28 * j + 28]], axis=1
            )
        rest = [last[10 * g:10 * g + 10, 84:100] for g in range(5)]
        out_ref[t, 150:160, :] = jnp.concatenate(rest + [jnp.zeros((10, 48), jnp.float32)], axis=1)


def multiply(m, amp, blocks, bd):
    return pl.pallas_call(
        product_kernel,
        in_specs=[pl.BlockSpec(memory_space=pltpu.SMEM)] + [pl.BlockSpec(memory_space=pltpu.VMEM)] * 6,
        out_specs=pl.BlockSpec(memory_space=pltpu.VMEM),
        scratch_shapes=[
            pltpu.VMEM((NA * C, 2 * Q), jnp.bfloat16),
            pltpu.VMEM((2, NP * WIDE, 2 * D * Q), jnp.bfloat16),
            pltpu.VMEM((8 * HALF, 2 * D * Q), jnp.bfloat16),
            pltpu.VMEM((8 * HALF, NP * WIDE), jnp.float32),
        ],
        out_shape=jax.ShapeDtypeStruct((8, PIECE, 128), jnp.float32),
        compiler_params=pltpu.CompilerParams(vmem_limit_bytes=32 * MIB),
        cost_estimate=pl.CostEstimate(flops=2 * 2 * 400 * 400 * 2048, bytes_accessed=6 * MIB, transcendentals=0),
        name="multiply",
    )(m, amp, *blocks, bd)


def last_kernel(parts_ref, out_ref, sum_ref):
    sum_ref[...] = jnp.sum(parts_ref[...].astype(jnp.float32), axis=0)
    for j in range(3):
        out_ref[:, j, :] = sum_ref[50 * j:50 * j + 50, 0:NA]
    rest = jnp.concatenate([sum_ref[150:160, 16 * g:16 * (g + 1)] for g in range(5)], axis=0)
    out_ref[:, 3, :] = jnp.concatenate([sum_ref[50 * j:50 * j + 50, NA:] for j in range(3)] + [rest], axis=1)


def finish(parts):
    return pl.pallas_call(
        last_kernel,
        in_specs=[pl.BlockSpec(memory_space=pltpu.VMEM)],
        out_specs=pl.BlockSpec(memory_space=pltpu.VMEM),
        out_shape=jax.ShapeDtypeStruct((50, NP, NA), jnp.float32),
        scratch_shapes=[pltpu.VMEM((PIECE, 128), jnp.float32)],
        compiler_params=pltpu.CompilerParams(vmem_limit_bytes=16 * MIB),
        name="finish",
    )(parts)


def home(z, delta):
    two = 2 if (z - delta) % 2 == 0 else -2
    return (z - (0, 1, two, -1)[delta]) % 16


def on_device(fitted_ac, fitted_bd, amplitudes):
    core, zl = (lax.axis_index(name) for name in ("core", "zl"))
    ways = []
    for f in range(4):
        for z in range(16):
            delta = (z - f) % 4
            ways.append((16 * f + z, 32 * HALF_OF[delta] + 16 * (z % 2) + home(z, delta)))
    shard = lax.ppermute(fitted_bd, ("xl", "core", "zq", "zl"), ways)
    amp = amplitudes.reshape(NP, D)
    peer = lax.ppermute(amp, "core", [(0, 1), (1, 0)])
    bd = lax.all_to_all(make_unit(core.astype(jnp.int32)[None], shard, amp, peer), ("yl", "xh", "xl"), 0, 0, tiled=True)
    ac = fitted_ac.reshape(NA * C, Q)
    blocks = {}
    for h in range(2):
        for m in range(2):
            ways = [(16 * e + z, 16 * (z % 2) + home(z, DELTA[h][e ^ m])) for e in range(2) for z in range(16)]
            blocks[h, m] = lax.ppermute(ac, ("core", "zq", "zl"), ways)
    blocks = [blocks[h, m] for h in range(2) for m in range(2)]
    amp = bd[:, NB, :2 * D * NP].reshape(C, D * NP)

    m = (zl % 2).astype(jnp.int32)[None]
    for_other = multiply(m ^ 1, amp, blocks, bd)
    for_self = multiply(m, amp, blocks, bd)
    pieces = (for_self + lax.ppermute(for_other, "core", [(0, 1), (1, 0)])).astype(jnp.bfloat16)
    summed = finish(lax.all_to_all(pieces, ("zq", "yh"), 0, 0, tiled=True))
    return jnp.transpose(summed, (1, 2, 0))


def solution(mesh):
    fine = Mesh(mesh.devices.reshape(2, 2, 2, 2, 4, 4, 2), ROW + COL)
    return jax.shard_map(
        on_device,
        mesh=fine,
        in_specs=(P(ROW, None, COL), P(ROW, None, COL), P(None, ROW, None)),
        out_specs=P(None, ROW, COL),
        check_vma=False,
    )
```

```python
import jax
import jax.numpy as jnp
from jax import lax
from jax.experimental import pallas as pl
from jax.experimental.pallas import tpu as pltpu
from jax.sharding import Mesh, PartitionSpec as P

ROW = ("yl", "xh", "xl", "core")
COL = ("zq", "zl", "yh")
DELTA = ((2, 1), (0, 3))
HALF_OF = (1, 0, 0, 1)
NT = (((1,), (1,)), ((), ()))
MIB = 1024 * 1024

NA, NB, C, D, NP, Q = 100, 100, 16, 8, 4, 128
ROWS = NA * NP
HALF = 50
UNIT = 104
WIDE = 128
PIECE = 160


def spread(amp, wide):
    tall, across = D * NP * wide, wide * C
    row = lax.broadcasted_iota(jnp.int32, (tall, D * NP), 0)
    col = lax.broadcasted_iota(jnp.int32, (tall, D * NP), 1)
    pick_row = jnp.where(row // wide == col, 1.0, 0.0).astype(jnp.bfloat16)
    row = lax.broadcasted_iota(jnp.int32, (C, across), 0)
    col = lax.broadcasted_iota(jnp.int32, (C, across), 1)
    pick_col = jnp.where(col % C == row, 1.0, 0.0).astype(jnp.bfloat16)
    wider = jnp.dot(pick_row, amp.T, preferred_element_type=jnp.float32).astype(jnp.bfloat16)
    full = jnp.dot(wider, pick_col, preferred_element_type=jnp.float32)
    row = lax.broadcasted_iota(jnp.int32, (tall, across), 0)
    col = lax.broadcasted_iota(jnp.int32, (tall, across), 1)
    return jnp.where(row % wide == col // C, full, 0.0).astype(jnp.bfloat16)


def in_a_row(amp):
    row = lax.broadcasted_iota(jnp.int32, (D, D * NP), 0)
    col = lax.broadcasted_iota(jnp.int32, (D, D * NP), 1)
    pick = jnp.where(col // NP == row, 1.0, 0.0).astype(jnp.bfloat16)
    wide = jnp.dot(amp, pick, preferred_element_type=jnp.float32)
    row = lax.broadcasted_iota(jnp.int32, (NP, D * NP), 0)
    col = lax.broadcasted_iota(jnp.int32, (NP, D * NP), 1)
    return jnp.sum(jnp.where(col % NP == row, wide, 0.0), axis=0, keepdims=True)


def unit_kernel(core_ref, bd_ref, amp_ref, peer_ref, out_ref, wide_ref, unit_ref, sem_ref):
    wide_ref[...] = bd_ref[...].astype(jnp.float32).reshape(NB * D, Q)
    for d in range(D):
        unit_ref[0:NB, d * Q:(d + 1) * Q] = wide_ref[pl.ds(d, NB, stride=D), :].astype(jnp.bfloat16)
    unit_ref[NB:, :] = jnp.zeros((UNIT - NB, D * Q), jnp.bfloat16)
    own, peer = in_a_row(amp_ref[...].astype(jnp.bfloat16)), in_a_row(peer_ref[...])
    first = core_ref[0] == 0
    both = jnp.concatenate([jnp.where(first, own, peer), jnp.where(first, peer, own)], axis=1)
    unit_ref[NB:NB + 1, 0:2 * D * NP] = both.astype(jnp.bfloat16)
    copies = [pltpu.make_async_copy(unit_ref, out_ref.at[t], sem_ref.at[t]) for t in range(8)]
    for copy in copies:
        copy.start()
    for copy in copies:
        copy.wait()


def make_unit(core, bd, amp, peer):
    inside, outside = pl.BlockSpec(memory_space=pltpu.VMEM), pl.BlockSpec(memory_space=pl.ANY)
    return pl.pallas_call(
        unit_kernel,
        in_specs=[pl.BlockSpec(memory_space=pltpu.SMEM), inside, inside, inside],
        out_specs=outside,
        out_shape=jax.ShapeDtypeStruct((8, UNIT, D * Q), jnp.bfloat16),
        scratch_shapes=[
            pltpu.VMEM((NB * D, Q), jnp.float32),
            pltpu.VMEM((UNIT, D * Q), jnp.bfloat16),
            pltpu.SemaphoreType.DMA((8,)),
        ],
        compiler_params=pltpu.CompilerParams(vmem_limit_bytes=16 * MIB),
        name="make_unit",
    )(core, bd, amp, peer)


def product_kernel(m_ref, amp_ref, ac00_ref, ac01_ref, ac10_ref, ac11_ref, bd_ref, out_ref, ac_ref, x_ref, left_ref, acc_ref):
    for m, pair in enumerate(((ac00_ref, ac10_ref), (ac01_ref, ac11_ref))):

        @pl.when(m_ref[0] == m)
        def _():
            for h in range(2):
                ac_ref[:, h * Q:(h + 1) * Q] = pair[h][...]

    for h in range(2):
        for t in range(4):
            left_ref[NB * t:NB * (t + 1), h * D * Q:(h + 1) * D * Q] = bd_ref[2 * t + h, 0:NB, :]
    w16, w4 = spread(amp_ref[...], 16), spread(amp_ref[...], 4)
    for k in range(7):
        w, n = (w16, 16) if k < 6 else (w4, 4)
        y = jnp.dot(w, ac_ref[k * 256:k * 256 + n * C, :], preferred_element_type=jnp.float32)
        high = y.astype(jnp.bfloat16)
        low = (y - high.astype(jnp.float32)).astype(jnp.bfloat16)
        for h in range(2):
            for d in range(D):
                for p in range(NP):
                    rows, columns = slice(WIDE * p + 16 * k, WIDE * p + 16 * k + n), slice((h * D + d) * Q, (h * D + d + 1) * Q)
                    here = slice(n * (d * NP + p), n * (d * NP + p + 1)), slice(Q * h, Q * (h + 1))
                    x_ref[0, rows, columns] = high[here]
                    x_ref[1, rows, columns] = low[here]
    acc_ref[...] = lax.dot_general(left_ref[...], x_ref[0], NT, preferred_element_type=jnp.float32) + lax.dot_general(
        left_ref[...], x_ref[1], NT, preferred_element_type=jnp.float32
    )
    for t in range(8):
        at = slice(HALF * t, HALF * (t + 1))
        last = acc_ref[at, 3 * WIDE:3 * WIDE + NA]
        for j in range(3):
            out_ref[t, 50 * j:50 * j + 50, :] = jnp.concatenate(
                [acc_ref[at, WIDE * j:WIDE * j + NA], last[:, 28 * j:28 * j + 28]], axis=1
            )
        rest = [last[10 * g:10 * g + 10, 84:100] for g in range(5)]
        out_ref[t, 150:160, :] = jnp.concatenate(rest + [jnp.zeros((10, 48), jnp.float32)], axis=1)


def multiply(m, amp, blocks, bd):
    return pl.pallas_call(
        product_kernel,
        in_specs=[pl.BlockSpec(memory_space=pltpu.SMEM)] + [pl.BlockSpec(memory_space=pltpu.VMEM)] * 6,
        out_specs=pl.BlockSpec(memory_space=pltpu.VMEM),
        scratch_shapes=[
            pltpu.VMEM((NA * C, 2 * Q), jnp.bfloat16),
            pltpu.VMEM((2, NP * WIDE, 2 * D * Q), jnp.bfloat16),
            pltpu.VMEM((8 * HALF, 2 * D * Q), jnp.bfloat16),
            pltpu.VMEM((8 * HALF, NP * WIDE), jnp.float32),
        ],
        out_shape=jax.ShapeDtypeStruct((8, PIECE, 128), jnp.float32),
        compiler_params=pltpu.CompilerParams(vmem_limit_bytes=32 * MIB),
        cost_estimate=pl.CostEstimate(flops=2 * 2 * 400 * 400 * 2048, bytes_accessed=6 * MIB, transcendentals=0),
        name="multiply",
    )(m, amp, *blocks, bd)


def last_kernel(parts_ref, out_ref, sum_ref):
    sum_ref[...] = jnp.sum(parts_ref[...].astype(jnp.float32), axis=0)
    for j in range(3):
        out_ref[:, j, :] = sum_ref[50 * j:50 * j + 50, 0:NA]
    rest = jnp.concatenate([sum_ref[150:160, 16 * g:16 * (g + 1)] for g in range(5)], axis=0)
    out_ref[:, 3, :] = jnp.concatenate([sum_ref[50 * j:50 * j + 50, NA:] for j in range(3)] + [rest], axis=1)


def finish(parts):
    return pl.pallas_call(
        last_kernel,
        in_specs=[pl.BlockSpec(memory_space=pltpu.VMEM)],
        out_specs=pl.BlockSpec(memory_space=pltpu.VMEM),
        out_shape=jax.ShapeDtypeStruct((50, NP, NA), jnp.float32),
        scratch_shapes=[pltpu.VMEM((PIECE, 128), jnp.float32)],
        compiler_params=pltpu.CompilerParams(vmem_limit_bytes=16 * MIB),
        name="finish",
    )(parts)


def home(z, delta):
    two = 2 if (z - delta) % 2 == 0 else -2
    return (z - (0, 1, two, -1)[delta]) % 16


def on_device(fitted_ac, fitted_bd, amplitudes):
    core, zl = (lax.axis_index(name) for name in ("core", "zl"))
    ways = []
    for f in range(4):
        for z in range(16):
            delta = (z - f) % 4
            ways.append((16 * f + z, 32 * HALF_OF[delta] + 16 * (z % 2) + home(z, delta)))
    shard = lax.ppermute(fitted_bd, ("xl", "core", "zq", "zl"), ways)
    amp = amplitudes.reshape(NP, D)
    peer = lax.ppermute(amp, "core", [(0, 1), (1, 0)])
    bd = lax.all_to_all(make_unit(core.astype(jnp.int32)[None], shard, amp.astype(jnp.float32), peer), ("yl", "xh", "xl"), 0, 0, tiled=True)
    ac = fitted_ac.reshape(NA * C, Q)
    blocks = {}
    for h in range(2):
        for m in range(2):
            ways = [(16 * e + z, 16 * (z % 2) + home(z, DELTA[h][e ^ m])) for e in range(2) for z in range(16)]
            blocks[h, m] = lax.ppermute(ac, ("core", "zq", "zl"), ways)
    blocks = [blocks[h, m] for h in range(2) for m in range(2)]
    amp = bd[:, NB, :2 * D * NP].reshape(C, D * NP)

    m = (zl % 2).astype(jnp.int32)[None]
    for_other = multiply(m ^ 1, amp, blocks, bd)
    for_self = multiply(m, amp, blocks, bd)
    pieces = (for_self + lax.ppermute(for_other, "core", [(0, 1), (1, 0)])).astype(jnp.bfloat16)
    summed = finish(lax.all_to_all(pieces, ("zq", "yh"), 0, 0, tiled=True))
    return jnp.transpose(summed, (1, 2, 0))


def solution(mesh):
    fine = Mesh(mesh.devices.reshape(2, 2, 2, 2, 4, 4, 2), ROW + COL)
    return jax.shard_map(
        on_device,
        mesh=fine,
        in_specs=(P(ROW, None, COL), P(ROW, None, COL), P(None, ROW, None)),
        out_specs=P(None, ROW, COL),
        check_vma=False,
    )
```

```python
import jax
import jax.numpy as jnp
from jax import lax
from jax.experimental import pallas as pl
from jax.experimental.pallas import tpu as pltpu
from jax.sharding import Mesh, PartitionSpec as P

ROW = ("yl", "xh", "xl", "core")
COL = ("zq", "zl", "yh")
ORDER = (2, 3, 0, 1)
DELTA = ((2, 1), (0, 3))
HALF_OF = (1, 0, 0, 1)
NT = (((1,), (1,)), ((), ()))
MIB = 1024 * 1024

NA, NB, C, D, NP, Q = 100, 100, 16, 8, 4, 128
ROWS = NA * NP
HALF = 50
UNIT = 104
WIDE = 128
PIECE = 160


def spread(amp, wide):
    tall, across = D * NP * wide, wide * C
    row = lax.broadcasted_iota(jnp.int32, (tall, D * NP), 0)
    col = lax.broadcasted_iota(jnp.int32, (tall, D * NP), 1)
    pick_row = jnp.where(row // wide == col, 1.0, 0.0).astype(jnp.bfloat16)
    row = lax.broadcasted_iota(jnp.int32, (C, across), 0)
    col = lax.broadcasted_iota(jnp.int32, (C, across), 1)
    pick_col = jnp.where(col % C == row, 1.0, 0.0).astype(jnp.bfloat16)
    wider = jnp.dot(pick_row, amp.T, preferred_element_type=jnp.float32).astype(jnp.bfloat16)
    full = jnp.dot(wider, pick_col, preferred_element_type=jnp.float32)
    row = lax.broadcasted_iota(jnp.int32, (tall, across), 0)
    col = lax.broadcasted_iota(jnp.int32, (tall, across), 1)
    return jnp.where(row % wide == col // C, full, 0.0).astype(jnp.bfloat16)


def in_a_row(amp):
    row = lax.broadcasted_iota(jnp.int32, (D, D * NP), 0)
    col = lax.broadcasted_iota(jnp.int32, (D, D * NP), 1)
    pick = jnp.where(col // NP == row, 1.0, 0.0).astype(jnp.bfloat16)
    wide = jnp.dot(amp, pick, preferred_element_type=jnp.float32)
    row = lax.broadcasted_iota(jnp.int32, (NP, D * NP), 0)
    col = lax.broadcasted_iota(jnp.int32, (NP, D * NP), 1)
    return jnp.sum(jnp.where(col % NP == row, wide, 0.0), axis=0, keepdims=True)


def unit_kernel(core_ref, bd_ref, amp_ref, peer_ref, out_ref, wide_ref, unit_ref, sem_ref):
    wide_ref[...] = bd_ref[...].astype(jnp.float32).reshape(NB * D, Q)
    for d in range(D):
        unit_ref[0:NB, d * Q:(d + 1) * Q] = wide_ref[pl.ds(d, NB, stride=D), :].astype(jnp.bfloat16)
    unit_ref[NB:, :] = jnp.zeros((UNIT - NB, D * Q), jnp.bfloat16)
    own, peer = in_a_row(amp_ref[...].astype(jnp.bfloat16)), in_a_row(peer_ref[...])
    first = core_ref[0] == 0
    both = jnp.concatenate([jnp.where(first, own, peer), jnp.where(first, peer, own)], axis=1)
    unit_ref[NB:NB + 1, 0:2 * D * NP] = both.astype(jnp.bfloat16)
    copies = [pltpu.make_async_copy(unit_ref, out_ref.at[t], sem_ref.at[t]) for t in range(8)]
    for copy in copies:
        copy.start()
    for copy in copies:
        copy.wait()


def make_unit(core, bd, amp, peer):
    inside, outside = pl.BlockSpec(memory_space=pltpu.VMEM), pl.BlockSpec(memory_space=pl.ANY)
    return pl.pallas_call(
        unit_kernel,
        in_specs=[pl.BlockSpec(memory_space=pltpu.SMEM), inside, inside, inside],
        out_specs=outside,
        out_shape=jax.ShapeDtypeStruct((8, UNIT, D * Q), jnp.bfloat16),
        scratch_shapes=[
            pltpu.VMEM((NB * D, Q), jnp.float32),
            pltpu.VMEM((UNIT, D * Q), jnp.bfloat16),
            pltpu.SemaphoreType.DMA((8,)),
        ],
        compiler_params=pltpu.CompilerParams(vmem_limit_bytes=16 * MIB),
        name="make_unit",
    )(core, bd, amp, peer)


def product_kernel(m_ref, amp_ref, ac00_ref, ac01_ref, ac10_ref, ac11_ref, bd_ref, out_ref, ac_ref, x_ref, left_ref, acc_ref):
    for m, pair in enumerate(((ac00_ref, ac10_ref), (ac01_ref, ac11_ref))):

        @pl.when(m_ref[0] == m)
        def _():
            for h in range(2):
                ac_ref[:, h * Q:(h + 1) * Q] = pair[h][...]

    for h in range(2):
        for t in range(4):
            left_ref[NB * t:NB * (t + 1), h * D * Q:(h + 1) * D * Q] = bd_ref[2 * t + h, 0:NB, :]
    w16, w4 = spread(amp_ref[...], 16), spread(amp_ref[...], 4)
    for k in range(7):
        w, n = (w16, 16) if k < 6 else (w4, 4)
        y = jnp.dot(w, ac_ref[k * 256:k * 256 + n * C, :], preferred_element_type=jnp.float32)
        high = y.astype(jnp.bfloat16)
        low = (y - high.astype(jnp.float32)).astype(jnp.bfloat16)
        for h in range(2):
            for d in range(D):
                for p in range(NP):
                    rows, columns = slice(WIDE * p + 16 * k, WIDE * p + 16 * k + n), slice((h * D + d) * Q, (h * D + d + 1) * Q)
                    here = slice(n * (d * NP + p), n * (d * NP + p + 1)), slice(Q * h, Q * (h + 1))
                    x_ref[0, rows, columns] = high[here]
                    x_ref[1, rows, columns] = low[here]
    acc_ref[...] = lax.dot_general(left_ref[...], x_ref[0], NT, preferred_element_type=jnp.float32) + lax.dot_general(
        left_ref[...], x_ref[1], NT, preferred_element_type=jnp.float32
    )
    for t in range(8):
        at = slice(HALF * t, HALF * (t + 1))
        to = 2 * ORDER.index(t // 2) + t % 2
        last = acc_ref[at, 3 * WIDE:3 * WIDE + NA]
        for j in range(3):
            out_ref[to, 50 * j:50 * j + 50, :] = jnp.concatenate(
                [acc_ref[at, WIDE * j:WIDE * j + NA], last[:, 28 * j:28 * j + 28]], axis=1
            )
        rest = [last[10 * g:10 * g + 10, 84:100] for g in range(5)]
        out_ref[to, 150:160, :] = jnp.concatenate(rest + [jnp.zeros((10, 48), jnp.float32)], axis=1)


def multiply(m, amp, blocks, bd):
    return pl.pallas_call(
        product_kernel,
        in_specs=[pl.BlockSpec(memory_space=pltpu.SMEM)] + [pl.BlockSpec(memory_space=pltpu.VMEM)] * 6,
        out_specs=pl.BlockSpec(memory_space=pltpu.VMEM),
        scratch_shapes=[
            pltpu.VMEM((NA * C, 2 * Q), jnp.bfloat16),
            pltpu.VMEM((2, NP * WIDE, 2 * D * Q), jnp.bfloat16),
            pltpu.VMEM((8 * HALF, 2 * D * Q), jnp.bfloat16),
            pltpu.VMEM((8 * HALF, NP * WIDE), jnp.float32),
        ],
        out_shape=jax.ShapeDtypeStruct((8, PIECE, 128), jnp.float32),
        compiler_params=pltpu.CompilerParams(vmem_limit_bytes=32 * MIB),
        cost_estimate=pl.CostEstimate(flops=2 * 2 * 400 * 400 * 2048, bytes_accessed=6 * MIB, transcendentals=0),
        name="multiply",
    )(m, amp, *blocks, bd)


def last_kernel(parts_ref, out_ref, sum_ref):
    sum_ref[...] = jnp.sum(parts_ref[...].astype(jnp.float32), axis=0)
    for j in range(3):
        out_ref[:, j, :] = sum_ref[50 * j:50 * j + 50, 0:NA]
    rest = jnp.concatenate([sum_ref[150:160, 16 * g:16 * (g + 1)] for g in range(5)], axis=0)
    out_ref[:, 3, :] = jnp.concatenate([sum_ref[50 * j:50 * j + 50, NA:] for j in range(3)] + [rest], axis=1)


def finish(parts):
    return pl.pallas_call(
        last_kernel,
        in_specs=[pl.BlockSpec(memory_space=pltpu.VMEM)],
        out_specs=pl.BlockSpec(memory_space=pltpu.VMEM),
        out_shape=jax.ShapeDtypeStruct((50, NP, NA), jnp.float32),
        scratch_shapes=[pltpu.VMEM((PIECE, 128), jnp.float32)],
        compiler_params=pltpu.CompilerParams(vmem_limit_bytes=16 * MIB),
        name="finish",
    )(parts)


def home(z, delta):
    two = 2 if (z - delta) % 2 == 0 else -2
    return (z - (0, 1, two, -1)[delta]) % 16


def on_device(fitted_ac, fitted_bd, amplitudes):
    core, zl = (lax.axis_index(name) for name in ("core", "zl"))
    ways = []
    for f in range(4):
        for z in range(16):
            delta = (z - f) % 4
            ways.append((16 * f + z, 32 * HALF_OF[delta] + 16 * (z % 2) + home(z, delta)))
    shard = lax.ppermute(fitted_bd, ("xl", "core", "zq", "zl"), ways)
    amp = amplitudes.reshape(NP, D)
    peer = lax.ppermute(amp, "core", [(0, 1), (1, 0)])
    bd = lax.all_to_all(make_unit(core.astype(jnp.int32)[None], shard, amp.astype(jnp.float32), peer), ("yl", "xh", "xl"), 0, 0, tiled=True)
    ac = fitted_ac.reshape(NA * C, Q)
    blocks = {}
    for h in range(2):
        for m in range(2):
            ways = [(16 * e + z, 16 * (z % 2) + home(z, DELTA[h][e ^ m])) for e in range(2) for z in range(16)]
            blocks[h, m] = lax.ppermute(ac, ("core", "zq", "zl"), ways)
    blocks = [blocks[h, m] for h in range(2) for m in range(2)]
    amp = bd[:, NB, :2 * D * NP].reshape(C, D * NP)

    m = (zl % 2).astype(jnp.int32)[None]
    for_other = multiply(m ^ 1, amp, blocks, bd)
    for_self = multiply(m, amp, blocks, bd)
    pieces = (for_self + lax.ppermute(for_other, "core", [(0, 1), (1, 0)])).astype(jnp.bfloat16)
    groups = [[8 * zq + 2 * f + y for zq in ORDER for y in range(2)] for f in range(4)]
    summed = finish(lax.all_to_all(pieces, COL, 0, 0, axis_index_groups=groups, tiled=True))
    return jnp.transpose(summed, (1, 2, 0))


def solution(mesh):
    fine = Mesh(mesh.devices.reshape(2, 2, 2, 2, 4, 4, 2), ROW + COL)
    return jax.shard_map(
        on_device,
        mesh=fine,
        in_specs=(P(ROW, None, COL), P(ROW, None, COL), P(None, ROW, None)),
        out_specs=P(None, ROW, COL),
        check_vma=False,
    )
```

```python
import jax
import jax.numpy as jnp
from jax import lax
from jax.experimental import pallas as pl
from jax.experimental.pallas import tpu as pltpu
from jax.sharding import Mesh, PartitionSpec as P

ROW = ("yl", "xh", "xl", "core")
COL = ("zq", "zl", "yh")
ORDER = (2, 3, 0, 1)
DELTA = ((2, 1), (0, 3))
HALF_OF = (1, 0, 0, 1)
NT = (((1,), (1,)), ((), ()))
MIB = 1024 * 1024

NA, NB, C, D, NP, Q = 100, 100, 16, 8, 4, 128
ROWS = NA * NP
HALF = 50
UNIT = 104
WIDE = 128
PIECE = 160


def spread(amp, wide):
    tall, across = D * NP * wide, wide * C
    row = lax.broadcasted_iota(jnp.int32, (tall, D * NP), 0)
    col = lax.broadcasted_iota(jnp.int32, (tall, D * NP), 1)
    pick_row = jnp.where(row // wide == col, 1.0, 0.0).astype(jnp.bfloat16)
    row = lax.broadcasted_iota(jnp.int32, (C, across), 0)
    col = lax.broadcasted_iota(jnp.int32, (C, across), 1)
    pick_col = jnp.where(col % C == row, 1.0, 0.0).astype(jnp.bfloat16)
    wider = jnp.dot(pick_row, amp.T, preferred_element_type=jnp.float32).astype(jnp.bfloat16)
    full = jnp.dot(wider, pick_col, preferred_element_type=jnp.float32)
    row = lax.broadcasted_iota(jnp.int32, (tall, across), 0)
    col = lax.broadcasted_iota(jnp.int32, (tall, across), 1)
    return jnp.where(row % wide == col // C, full, 0.0).astype(jnp.bfloat16)


def in_a_row(amp):
    row = lax.broadcasted_iota(jnp.int32, (D, D * NP), 0)
    col = lax.broadcasted_iota(jnp.int32, (D, D * NP), 1)
    pick = jnp.where(col // NP == row, 1.0, 0.0).astype(jnp.bfloat16)
    wide = jnp.dot(amp, pick, preferred_element_type=jnp.float32)
    row = lax.broadcasted_iota(jnp.int32, (NP, D * NP), 0)
    col = lax.broadcasted_iota(jnp.int32, (NP, D * NP), 1)
    return jnp.sum(jnp.where(col % NP == row, wide, 0.0), axis=0, keepdims=True)


def unit_kernel(core_ref, bd_ref, amp_ref, peer_ref, out_ref, wide_ref, unit_ref, sem_ref):
    wide_ref[...] = bd_ref[...].astype(jnp.float32).reshape(NB * D, Q)
    for d in range(D):
        unit_ref[0:NB, d * Q:(d + 1) * Q] = wide_ref[pl.ds(d, NB, stride=D), :].astype(jnp.bfloat16)
    unit_ref[NB:, :] = jnp.zeros((UNIT - NB, D * Q), jnp.bfloat16)
    own, peer = in_a_row(amp_ref[...].astype(jnp.bfloat16)), in_a_row(peer_ref[...])
    first = core_ref[0] == 0
    both = jnp.concatenate([jnp.where(first, own, peer), jnp.where(first, peer, own)], axis=1)
    unit_ref[NB:NB + 1, 0:2 * D * NP] = both.astype(jnp.bfloat16)
    copies = [pltpu.make_async_copy(unit_ref, out_ref.at[t], sem_ref.at[t]) for t in range(8)]
    for copy in copies:
        copy.start()
    for copy in copies:
        copy.wait()


def make_unit(core, bd, amp, peer):
    inside, outside = pl.BlockSpec(memory_space=pltpu.VMEM), pl.BlockSpec(memory_space=pl.ANY)
    return pl.pallas_call(
        unit_kernel,
        in_specs=[pl.BlockSpec(memory_space=pltpu.SMEM), inside, inside, inside],
        out_specs=outside,
        out_shape=jax.ShapeDtypeStruct((8, UNIT, D * Q), jnp.bfloat16),
        scratch_shapes=[
            pltpu.VMEM((NB * D, Q), jnp.float32),
            pltpu.VMEM((UNIT, D * Q), jnp.bfloat16),
            pltpu.SemaphoreType.DMA((8,)),
        ],
        compiler_params=pltpu.CompilerParams(vmem_limit_bytes=16 * MIB),
        name="make_unit",
    )(core, bd, amp, peer)


def product_kernel(m_ref, amp_ref, ac00_ref, ac01_ref, ac10_ref, ac11_ref, bd_ref, out_ref, ac_ref, x_ref, left_ref, acc_ref):
    for m, pair in enumerate(((ac00_ref, ac10_ref), (ac01_ref, ac11_ref))):

        @pl.when(m_ref[0] == m)
        def _():
            for h in range(2):
                ac_ref[:, h * Q:(h + 1) * Q] = pair[h][...]

    for h in range(2):
        for t in range(4):
            left_ref[NB * t:NB * (t + 1), h * D * Q:(h + 1) * D * Q] = bd_ref[2 * t + h, 0:NB, :]
    w16, w4 = spread(amp_ref[...], 16), spread(amp_ref[...], 4)
    for k in range(7):
        w, n = (w16, 16) if k < 6 else (w4, 4)
        y = jnp.dot(w, ac_ref[k * 256:k * 256 + n * C, :], preferred_element_type=jnp.float32)
        high = y.astype(jnp.bfloat16)
        low = (y - high.astype(jnp.float32)).astype(jnp.bfloat16)
        for h in range(2):
            for d in range(D):
                for p in range(NP):
                    rows, columns = slice(WIDE * p + 16 * k, WIDE * p + 16 * k + n), slice((h * D + d) * Q, (h * D + d + 1) * Q)
                    here = slice(n * (d * NP + p), n * (d * NP + p + 1)), slice(Q * h, Q * (h + 1))
                    x_ref[0, rows, columns] = high[here]
                    x_ref[1, rows, columns] = low[here]
    acc_ref[...] = lax.dot_general(left_ref[...], x_ref[0], NT, preferred_element_type=jnp.float32) + lax.dot_general(
        left_ref[...], x_ref[1], NT, preferred_element_type=jnp.float32
    )
    for t in range(8):
        at = slice(HALF * t, HALF * (t + 1))
        to = 2 * ORDER.index(t // 2) + 1 - t % 2
        last = acc_ref[at, 3 * WIDE:3 * WIDE + NA]
        for j in range(3):
            out_ref[to, 50 * j:50 * j + 50, :] = jnp.concatenate(
                [acc_ref[at, WIDE * j:WIDE * j + NA], last[:, 28 * j:28 * j + 28]], axis=1
            )
        rest = [last[10 * g:10 * g + 10, 84:100] for g in range(5)]
        out_ref[to, 150:160, :] = jnp.concatenate(rest + [jnp.zeros((10, 48), jnp.float32)], axis=1)


def multiply(m, amp, blocks, bd):
    return pl.pallas_call(
        product_kernel,
        in_specs=[pl.BlockSpec(memory_space=pltpu.SMEM)] + [pl.BlockSpec(memory_space=pltpu.VMEM)] * 6,
        out_specs=pl.BlockSpec(memory_space=pltpu.VMEM),
        scratch_shapes=[
            pltpu.VMEM((NA * C, 2 * Q), jnp.bfloat16),
            pltpu.VMEM((2, NP * WIDE, 2 * D * Q), jnp.bfloat16),
            pltpu.VMEM((8 * HALF, 2 * D * Q), jnp.bfloat16),
            pltpu.VMEM((8 * HALF, NP * WIDE), jnp.float32),
        ],
        out_shape=jax.ShapeDtypeStruct((8, PIECE, 128), jnp.float32),
        compiler_params=pltpu.CompilerParams(vmem_limit_bytes=32 * MIB),
        cost_estimate=pl.CostEstimate(flops=2 * 2 * 400 * 400 * 2048, bytes_accessed=6 * MIB, transcendentals=0),
        name="multiply",
    )(m, amp, *blocks, bd)


def last_kernel(parts_ref, out_ref, sum_ref):
    sum_ref[...] = jnp.sum(parts_ref[...].astype(jnp.float32), axis=0)
    for j in range(3):
        out_ref[:, j, :] = sum_ref[50 * j:50 * j + 50, 0:NA]
    rest = jnp.concatenate([sum_ref[150:160, 16 * g:16 * (g + 1)] for g in range(5)], axis=0)
    out_ref[:, 3, :] = jnp.concatenate([sum_ref[50 * j:50 * j + 50, NA:] for j in range(3)] + [rest], axis=1)


def finish(parts):
    return pl.pallas_call(
        last_kernel,
        in_specs=[pl.BlockSpec(memory_space=pltpu.VMEM)],
        out_specs=pl.BlockSpec(memory_space=pltpu.VMEM),
        out_shape=jax.ShapeDtypeStruct((50, NP, NA), jnp.float32),
        scratch_shapes=[pltpu.VMEM((PIECE, 128), jnp.float32)],
        compiler_params=pltpu.CompilerParams(vmem_limit_bytes=16 * MIB),
        name="finish",
    )(parts)


def home(z, delta):
    two = -2 if (z - delta) % 2 == 0 else 2
    return (z - (0, 1, two, -1)[delta]) % 16


def on_device(fitted_ac, fitted_bd, amplitudes):
    core, zl = (lax.axis_index(name) for name in ("core", "zl"))
    ways = []
    for f in range(4):
        for z in range(16):
            delta = (z - f) % 4
            ways.append((16 * f + z, 32 * HALF_OF[delta] + 16 * (z % 2) + home(z, delta)))
    shard = lax.ppermute(fitted_bd, ("xl", "core", "zq", "zl"), ways)
    amp = amplitudes.reshape(NP, D)
    peer = lax.ppermute(amp, "core", [(0, 1), (1, 0)])
    bd = lax.all_to_all(make_unit(core.astype(jnp.int32)[None], shard, amp.astype(jnp.float32), peer), ("yl", "xh", "xl"), 0, 0, tiled=True)
    ac = fitted_ac.reshape(NA * C, Q)
    blocks = {}
    for h in range(2):
        for m in range(2):
            ways = [(16 * e + z, 16 * (z % 2) + home(z, DELTA[h][e ^ m])) for e in range(2) for z in range(16)]
            blocks[h, m] = lax.ppermute(ac, ("core", "zq", "zl"), ways)
    blocks = [blocks[h, m] for h in range(2) for m in range(2)]
    amp = bd[:, NB, :2 * D * NP].reshape(C, D * NP)

    m = (zl % 2).astype(jnp.int32)[None]
    for_other = multiply(m ^ 1, amp, blocks, bd)
    for_self = multiply(m, amp, blocks, bd)
    pieces = (for_self + lax.ppermute(for_other, "core", [(0, 1), (1, 0)])).astype(jnp.bfloat16)
    groups = [[8 * zq + 2 * f + y for zq in ORDER for y in (1, 0)] for f in range(4)]
    summed = finish(lax.all_to_all(pieces, COL, 0, 0, axis_index_groups=groups, tiled=True))
    return jnp.transpose(summed, (1, 2, 0))


def solution(mesh):
    fine = Mesh(mesh.devices.reshape(2, 2, 2, 2, 4, 4, 2), ROW + COL)
    return jax.shard_map(
        on_device,
        mesh=fine,
        in_specs=(P(ROW, None, COL), P(ROW, None, COL), P(None, ROW, None)),
        out_specs=P(None, ROW, COL),
        check_vma=False,
    )
```

```python
import jax
import jax.numpy as jnp
from jax import lax
from jax.experimental import pallas as pl
from jax.experimental.pallas import tpu as pltpu
from jax.sharding import Mesh, PartitionSpec as P

ROW = ("yl", "xh", "xl", "core")
COL = ("zq", "zl", "yh")
FLIP = 6
ORDER = (2, 3, 0, 1)
DELTA = ((2, 1), (0, 3))
HALF_OF = (1, 0, 0, 1)
NT = (((1,), (1,)), ((), ()))
MIB = 1024 * 1024

NA, NB, C, D, NP, Q = 100, 100, 16, 8, 4, 128
ROWS = NA * NP
HALF = 50
UNIT = 104
WIDE = 128
PIECE = 160


def spread(amp, wide):
    tall, across = D * NP * wide, wide * C
    row = lax.broadcasted_iota(jnp.int32, (tall, D * NP), 0)
    col = lax.broadcasted_iota(jnp.int32, (tall, D * NP), 1)
    pick_row = jnp.where(row // wide == col, 1.0, 0.0).astype(jnp.bfloat16)
    row = lax.broadcasted_iota(jnp.int32, (C, across), 0)
    col = lax.broadcasted_iota(jnp.int32, (C, across), 1)
    pick_col = jnp.where(col % C == row ^ (2 * FLIP), 1.0, 0.0).astype(jnp.bfloat16)
    wider = jnp.dot(pick_row, amp.T, preferred_element_type=jnp.float32).astype(jnp.bfloat16)
    full = jnp.dot(wider, pick_col, preferred_element_type=jnp.float32)
    row = lax.broadcasted_iota(jnp.int32, (tall, across), 0)
    col = lax.broadcasted_iota(jnp.int32, (tall, across), 1)
    return jnp.where(row % wide == col // C, full, 0.0).astype(jnp.bfloat16)


def in_a_row(amp):
    row = lax.broadcasted_iota(jnp.int32, (D, D * NP), 0)
    col = lax.broadcasted_iota(jnp.int32, (D, D * NP), 1)
    pick = jnp.where(col // NP == row, 1.0, 0.0).astype(jnp.bfloat16)
    wide = jnp.dot(amp, pick, preferred_element_type=jnp.float32)
    row = lax.broadcasted_iota(jnp.int32, (NP, D * NP), 0)
    col = lax.broadcasted_iota(jnp.int32, (NP, D * NP), 1)
    return jnp.sum(jnp.where(col % NP == row, wide, 0.0), axis=0, keepdims=True)


def unit_kernel(core_ref, bd_ref, amp_ref, peer_ref, out_ref, wide_ref, unit_ref, sem_ref):
    wide_ref[...] = bd_ref[...].astype(jnp.float32).reshape(NB * D, Q)
    for d in range(D):
        unit_ref[0:NB, d * Q:(d + 1) * Q] = wide_ref[pl.ds(d, NB, stride=D), :].astype(jnp.bfloat16)
    unit_ref[NB:, :] = jnp.zeros((UNIT - NB, D * Q), jnp.bfloat16)
    own, peer = in_a_row(amp_ref[...].astype(jnp.bfloat16)), in_a_row(peer_ref[...])
    first = core_ref[0] == 0
    both = jnp.concatenate([jnp.where(first, own, peer), jnp.where(first, peer, own)], axis=1)
    unit_ref[NB:NB + 1, 0:2 * D * NP] = both.astype(jnp.bfloat16)
    copies = [pltpu.make_async_copy(unit_ref, out_ref.at[t], sem_ref.at[t]) for t in range(8)]
    for copy in copies:
        copy.start()
    for copy in copies:
        copy.wait()


def make_unit(core, bd, amp, peer):
    inside, outside = pl.BlockSpec(memory_space=pltpu.VMEM), pl.BlockSpec(memory_space=pl.ANY)
    return pl.pallas_call(
        unit_kernel,
        in_specs=[pl.BlockSpec(memory_space=pltpu.SMEM), inside, inside, inside],
        out_specs=outside,
        out_shape=jax.ShapeDtypeStruct((8, UNIT, D * Q), jnp.bfloat16),
        scratch_shapes=[
            pltpu.VMEM((NB * D, Q), jnp.float32),
            pltpu.VMEM((UNIT, D * Q), jnp.bfloat16),
            pltpu.SemaphoreType.DMA((8,)),
        ],
        compiler_params=pltpu.CompilerParams(vmem_limit_bytes=16 * MIB),
        name="make_unit",
    )(core, bd, amp, peer)


def product_kernel(m_ref, amp_ref, ac00_ref, ac01_ref, ac10_ref, ac11_ref, bd_ref, out_ref, ac_ref, x_ref, left_ref, acc_ref):
    for m, pair in enumerate(((ac00_ref, ac10_ref), (ac01_ref, ac11_ref))):

        @pl.when(m_ref[0] == m)
        def _():
            for h in range(2):
                ac_ref[:, h * Q:(h + 1) * Q] = pair[h][...]

    for h in range(2):
        for t in range(4):
            left_ref[NB * t:NB * (t + 1), h * D * Q:(h + 1) * D * Q] = bd_ref[(2 * t + h) ^ FLIP, 0:NB, :]
    w16, w4 = spread(amp_ref[...], 16), spread(amp_ref[...], 4)
    for k in range(7):
        w, n = (w16, 16) if k < 6 else (w4, 4)
        y = jnp.dot(w, ac_ref[k * 256:k * 256 + n * C, :], preferred_element_type=jnp.float32)
        high = y.astype(jnp.bfloat16)
        low = (y - high.astype(jnp.float32)).astype(jnp.bfloat16)
        for h in range(2):
            for d in range(D):
                for p in range(NP):
                    rows, columns = slice(WIDE * p + 16 * k, WIDE * p + 16 * k + n), slice((h * D + d) * Q, (h * D + d + 1) * Q)
                    here = slice(n * (d * NP + p), n * (d * NP + p + 1)), slice(Q * h, Q * (h + 1))
                    x_ref[0, rows, columns] = high[here]
                    x_ref[1, rows, columns] = low[here]
    acc_ref[...] = lax.dot_general(left_ref[...], x_ref[0], NT, preferred_element_type=jnp.float32) + lax.dot_general(
        left_ref[...], x_ref[1], NT, preferred_element_type=jnp.float32
    )
    for t in range(8):
        at = slice(HALF * t, HALF * (t + 1))
        to = 2 * ORDER.index(t // 2) + 1 - t % 2
        last = acc_ref[at, 3 * WIDE:3 * WIDE + NA]
        for j in range(3):
            out_ref[to, 50 * j:50 * j + 50, :] = jnp.concatenate(
                [acc_ref[at, WIDE * j:WIDE * j + NA], last[:, 28 * j:28 * j + 28]], axis=1
            )
        rest = [last[10 * g:10 * g + 10, 84:100] for g in range(5)]
        out_ref[to, 150:160, :] = jnp.concatenate(rest + [jnp.zeros((10, 48), jnp.float32)], axis=1)


def multiply(m, amp, blocks, bd):
    return pl.pallas_call(
        product_kernel,
        in_specs=[pl.BlockSpec(memory_space=pltpu.SMEM)] + [pl.BlockSpec(memory_space=pltpu.VMEM)] * 6,
        out_specs=pl.BlockSpec(memory_space=pltpu.VMEM),
        scratch_shapes=[
            pltpu.VMEM((NA * C, 2 * Q), jnp.bfloat16),
            pltpu.VMEM((2, NP * WIDE, 2 * D * Q), jnp.bfloat16),
            pltpu.VMEM((8 * HALF, 2 * D * Q), jnp.bfloat16),
            pltpu.VMEM((8 * HALF, NP * WIDE), jnp.float32),
        ],
        out_shape=jax.ShapeDtypeStruct((8, PIECE, 128), jnp.float32),
        compiler_params=pltpu.CompilerParams(vmem_limit_bytes=32 * MIB),
        cost_estimate=pl.CostEstimate(flops=2 * 2 * 400 * 400 * 2048, bytes_accessed=6 * MIB, transcendentals=0),
        name="multiply",
    )(m, amp, *blocks, bd)


def last_kernel(parts_ref, out_ref, sum_ref):
    sum_ref[...] = jnp.sum(parts_ref[...].astype(jnp.float32), axis=0)
    for j in range(3):
        out_ref[:, j, :] = sum_ref[50 * j:50 * j + 50, 0:NA]
    rest = jnp.concatenate([sum_ref[150:160, 16 * g:16 * (g + 1)] for g in range(5)], axis=0)
    out_ref[:, 3, :] = jnp.concatenate([sum_ref[50 * j:50 * j + 50, NA:] for j in range(3)] + [rest], axis=1)


def finish(parts):
    return pl.pallas_call(
        last_kernel,
        in_specs=[pl.BlockSpec(memory_space=pltpu.VMEM)],
        out_specs=pl.BlockSpec(memory_space=pltpu.VMEM),
        out_shape=jax.ShapeDtypeStruct((50, NP, NA), jnp.float32),
        scratch_shapes=[pltpu.VMEM((PIECE, 128), jnp.float32)],
        compiler_params=pltpu.CompilerParams(vmem_limit_bytes=16 * MIB),
        name="finish",
    )(parts)


def home(z, delta):
    two = -2 if (z - delta) % 2 == 0 else 2
    return (z - (0, 1, two, -1)[delta]) % 16


def on_device(fitted_ac, fitted_bd, amplitudes):
    core, zl = (lax.axis_index(name) for name in ("core", "zl"))
    ways = []
    for f in range(4):
        for z in range(16):
            delta = (z - f) % 4
            ways.append((16 * f + z, 32 * HALF_OF[delta] + 16 * (z % 2) + home(z, delta)))
    shard = lax.ppermute(fitted_bd, ("xl", "core", "zq", "zl"), ways)
    amp = amplitudes.reshape(NP, D)
    peer = lax.ppermute(amp, "core", [(0, 1), (1, 0)])
    bd = lax.all_to_all(make_unit(core.astype(jnp.int32)[None], shard, amp.astype(jnp.float32), peer), ("yl", "xh", "xl"), 0, 0, axis_index_groups=[[i ^ FLIP for i in range(8)]], tiled=True)
    ac = fitted_ac.reshape(NA * C, Q)
    blocks = {}
    for h in range(2):
        for m in range(2):
            ways = [(16 * e + z, 16 * (z % 2) + home(z, DELTA[h][e ^ m])) for e in range(2) for z in range(16)]
            blocks[h, m] = lax.ppermute(ac, ("core", "zq", "zl"), ways)
    blocks = [blocks[h, m] for h in range(2) for m in range(2)]
    amp = bd[:, NB, :2 * D * NP].reshape(C, D * NP)

    m = (zl % 2).astype(jnp.int32)[None]
    for_other = multiply(m ^ 1, amp, blocks, bd)
    for_self = multiply(m, amp, blocks, bd)
    pieces = (for_self + lax.ppermute(for_other, "core", [(0, 1), (1, 0)])).astype(jnp.bfloat16)
    groups = [[8 * zq + 2 * f + y for zq in ORDER for y in (1, 0)] for f in range(4)]
    summed = finish(lax.all_to_all(pieces, COL, 0, 0, axis_index_groups=groups, tiled=True))
    return jnp.transpose(summed, (1, 2, 0))


def solution(mesh):
    fine = Mesh(mesh.devices.reshape(2, 2, 2, 2, 4, 4, 2), ROW + COL)
    return jax.shard_map(
        on_device,
        mesh=fine,
        in_specs=(P(ROW, None, COL), P(ROW, None, COL), P(None, ROW, None)),
        out_specs=P(None, ROW, COL),
        check_vma=False,
    )
```
